32 devices in a mesh: blk: 8 (over z, x), mode: 4 (over y, core).
Axes of the slice: x: 2, y: 2, z: 4, core: 2. Of those that a mesh axis runs over, the one named last changes fastest.
Arguments:
- chaos_field: float32 [448, 32768], P('mode', 'blk'), may hold values from -6 to 6
- kl_field: float32 [13, 32768], P(None, 'blk'), may hold values from -1.6 to 4, as said below
- partner: int32 [12, 2, 448], P(None, None, 'mode'), may hold values from 0 to 447, each once within a row
- chaos_coef: float32 [12, 2, 448], P(None, None, 'mode'), may hold values from 0.5 to 2
- cell_count: int32 [8], P('blk'), may hold values from 2048 to 4096, as said below
- face_count: int32 [8, 4], P('blk'), may hold values from 0 to 128, as said below
- face_cells: int32 [8, 4, 128], P('blk'), may hold values from 0 to 4095, as said below
Outputs:
- applied: float32 [448, 32768], P('mode', 'blk')
The draws below stay inside these ranges and needn't reach their ends.
Inputs may be any that keep to these rules, and one draw needn't show every extreme that they name: A block's live cells are its first cell_count cells, a whole number of rows of 128; some block is full. `face_count`: slots are the neighbouring blocks at offsets -2, -1, +1, +2 of the block index; a pair of blocks has the same count seen from either side, and 0 where the neighbour does not exist. `face_cells`: entry f of a slot pairs with entry f of the neighbour's opposite slot; entries below the count name live cells. `kl_field`: row 0 lies in 0.5 to 4.
All inputs are finite; a program needn't handle non-finite values.
Results may differ from the reference program's by a relative error of at most 0.000068.
Values sent between devices are 32-bit elements; how exact they have to be, the bound alone decides.
A program may use at most 64 MiB of HBM per device.

```python
import math
import jax
import jax.numpy as jnp
from jax import lax

GX = 32
GZ = 128
MODES = 448
KL = 12
FACE_MAX = 128
NBLK = 8
CELLS = 32768


def block_layout(key):
    folded = jax.random.fold_in(key, 41)
    key_rows, key_full, key_count, key_pick, key_low, key_high = jax.random.split(folded, 6)
    block_ids = jnp.arange(NBLK, dtype=jnp.int32)
    grid_rows = jax.random.randint(key_rows, (NBLK,), GX // 2, GX + 1)
    full_block = jax.random.randint(key_full, (), 0, NBLK)
    grid_rows = jnp.where(block_ids == full_block, GX, grid_rows)
    alive_cells = (grid_rows * GZ).astype(jnp.int32)
    pair_count = jax.random.randint(key_count, (NBLK, 2), 0, FACE_MAX + 1)
    widest = jax.random.randint(key_pick, (), 0, NBLK - 1)
    pair_count = jnp.where((block_ids[:, None] == widest) & (jnp.arange(2)[None, :] == 0), FACE_MAX, pair_count)
    partner_ids = block_ids[:, None] + jnp.arange(1, 3, dtype=jnp.int32)[None, :]
    pair_count = jnp.where(partner_ids < NBLK, pair_count, 0).astype(jnp.int32)
    low_cells = jax.random.randint(key_low, (NBLK, 2, FACE_MAX), 0, 1 << 30) % alive_cells[:, None, None]
    partner_alive = alive_cells[jnp.minimum(partner_ids, NBLK - 1)]
    high_cells = jax.random.randint(key_high, (NBLK, 2, FACE_MAX), 0, 1 << 30) % partner_alive[:, :, None]
    return (alive_cells, pair_count, low_cells.astype(jnp.int32), high_cells.astype(jnp.int32))


def shift_down(values, distance):
    return jnp.concatenate([jnp.zeros_like(values[:distance]), values[:-distance]], axis=0)[:values.shape[0]]


def draw_cell_count(key, part):
    return block_layout(key)[0]


def draw_face_count(key, part):
    pair_count = block_layout(key)[1]
    return jnp.stack([shift_down(pair_count[:, 1], 2), shift_down(pair_count[:, 0], 1), pair_count[:, 0], pair_count[:, 1]], axis=1).astype(jnp.int32)


def draw_face_cells(key, part):
    layout = block_layout(key)
    low_cells = layout[2]
    high_cells = layout[3]
    return jnp.stack([shift_down(high_cells[:, 1], 2), shift_down(high_cells[:, 0], 1), low_cells[:, 0], low_cells[:, 1]], axis=1).astype(jnp.int32)


def draw_kl_field(key, part):
    key_mean, key_terms = jax.random.split(jax.random.fold_in(key, 5))
    mean_row = jnp.exp(jax.random.uniform(key_mean, (1, CELLS), jnp.float32, math.log(0.5), math.log(4.0)))
    term_rows = jnp.clip(0.4 * jax.random.normal(key_terms, (KL, CELLS), jnp.float32), -1.6, 1.6)
    return jnp.concatenate([mean_row, term_rows], axis=0).astype(jnp.float32)


def levels(key, shape, shards, smallest, high):
    loudness, own = 1.0, jax.random.fold_in(key, 6)
    for axis_at, blocks in shards:
        steps = jnp.exp(jax.random.uniform(jax.random.fold_in(own, axis_at), (blocks,), jnp.float32, smallest / len(shards), high / len(shards)))
        loudness = loudness * jnp.repeat(steps, shape[axis_at] // blocks).reshape([-1 if axis == axis_at else 1 for axis in range(len(shape))])
    return loudness


def scatter_about(stream_key, extent, spread, bound, shards=(), held_as=jnp.bfloat16):
    factor_of = levels(stream_key, extent, shards, -0.22, 0.18) if shards else 1.0
    drawn = jax.random.normal(stream_key, extent, jnp.float32) * spread * factor_of
    return jnp.minimum(jnp.maximum(drawn, -bound), bound).astype(held_as)


def setup_inputs(seed: int = 0) -> dict:
    arg_keys = jax.random.split(jax.random.key(seed), 8)
    chaos_field = scatter_about(arg_keys[0], (MODES, CELLS), 1.0, 6.0, ((0, 4), (1, 8)), jnp.float32)
    kl_field = draw_kl_field(jax.random.fold_in(arg_keys[7], 71), 0)
    partner = jax.vmap(lambda own: jax.random.permutation(own, MODES))(jax.random.split(arg_keys[2], KL * 2)).reshape((KL, 2, MODES)).astype(jnp.int32)
    chaos_coef = jnp.clip(0.5 + 1.5 * jax.random.uniform(arg_keys[3], (KL, 2, MODES), jnp.float32) ** levels(arg_keys[3], (KL, 2, MODES), ((2, 4),), -0.2, 0.2), 0.5, 2.0)
    cell_count = draw_cell_count(jax.random.fold_in(arg_keys[7], 71), 0)
    face_count = draw_face_count(jax.random.fold_in(arg_keys[7], 71), 0)
    face_cells = draw_face_cells(jax.random.fold_in(arg_keys[7], 71), 0)
    return dict(chaos_field=chaos_field, kl_field=kl_field, partner=partner, chaos_coef=chaos_coef, cell_count=cell_count, face_count=face_count, face_cells=face_cells)


SLOT_OFFSETS = (-2, -1, 1, 2)


def grid_terms(values, conduct, alive_grid):
    down_coef = 0.5 * (conduct[..., 1:, :] + conduct[..., :-1, :]) * (alive_grid[..., 1:, :] * alive_grid[..., :-1, :])
    down_step = down_coef * (values[..., :-1, :] - values[..., 1:, :])
    side_coef = 0.5 * (conduct[..., :, 1:] + conduct[..., :, :-1]) * (alive_grid[..., :, 1:] * alive_grid[..., :, :-1])
    side_step = side_coef * (values[..., :, :-1] - values[..., :, 1:])
    leading = [(0, 0)] * (values.ndim - 2)
    result = jnp.pad(down_step, leading + [(0, 1), (0, 0)]) - jnp.pad(down_step, leading + [(1, 0), (0, 0)])
    return result + jnp.pad(side_step, leading + [(0, 0), (0, 1)]) - jnp.pad(side_step, leading + [(0, 0), (1, 0)])


def reference(chaos_field, kl_field, partner, chaos_coef, cell_count, face_count, face_cells):
    cells_block = GX * GZ
    alive_flag = (lax.iota(jnp.int32, cells_block)[None, :] < cell_count[:, None]).astype(jnp.float32)
    alive_grid = alive_flag.reshape(NBLK, GX, GZ)
    alive_flat = alive_flag.reshape(1, -1)
    masked = chaos_field * alive_flat
    block_ids = jnp.arange(NBLK, dtype=jnp.int32)
    own_index = (block_ids[:, None, None] * cells_block + face_cells).reshape(-1).astype(jnp.int32)
    remote_list = []
    for slot_index, offset in enumerate(SLOT_OFFSETS):
        neighbour = jnp.clip(block_ids + offset, 0, NBLK - 1).astype(jnp.int32)
        remote_list.append(neighbour[:, None] * cells_block + face_cells[neighbour, 3 - slot_index])
    remote_index = jnp.stack(remote_list, axis=1).reshape(-1).astype(jnp.int32)
    face_alive = (lax.iota(jnp.int32, FACE_MAX)[None, None, :] < face_count[:, :, None]).astype(jnp.float32).reshape(-1)
    summed = jnp.zeros((MODES, CELLS), jnp.float32)
    for kl_index in range(KL + 1):
        if kl_index == 0:
            mixed_field = masked
        else:
            pairs = partner[kl_index - 1]
            weights = chaos_coef[kl_index - 1]
            mixed_field = weights[0][:, None] * masked[pairs[0]] + weights[1][:, None] * masked[pairs[1]]
        conduct = kl_field[kl_index]
        grid_part = grid_terms(mixed_field.reshape(MODES, NBLK, GX, GZ), conduct.reshape(NBLK, GX, GZ), alive_grid)
        face_coef = 0.5 * (conduct[own_index] + conduct[remote_index]) * face_alive
        face_part = face_coef[None, :] * (mixed_field[:, own_index] - mixed_field[:, remote_index])
        summed = summed + grid_part.reshape(MODES, CELLS)
        summed = summed.at[:, own_index].add(face_part)
    return summed * alive_flat
```

```python
import functools

import jax
import jax.numpy as jnp
from jax import lax
from jax.experimental import pallas as pl
from jax.experimental.pallas import tpu as pltpu
from jax.sharding import PartitionSpec as P

GZ = 128
ROWS = 8
CHUNK = ROWS * GZ
WIDE = 256
TOGETHER = 4
SLOT_OFFSETS = (-2, -1, 1, 2)
VMEM = pl.BlockSpec(memory_space=pltpu.VMEM)
SMEM = pl.BlockSpec(memory_space=pltpu.SMEM)


def params():
    return pltpu.CompilerParams(vmem_limit_bytes=32 * 1024 * 1024)


def cost(flops, size):
    return pl.CostEstimate(flops=flops, bytes_accessed=size, transcendentals=0)


def shifted(value, axis, steps):
    count = lax.axis_size(axis)
    first, last = (max(0, -steps), min(count, count - steps))
    return lax.ppermute(value, axis, [(source, source + steps) for source in range(first, last)])


def split_rows(value):
    high = value.astype(jnp.bfloat16)
    rest = value - high.astype(jnp.float32)
    middle = rest.astype(jnp.bfloat16)
    low = (rest - middle.astype(jnp.float32)).astype(jnp.bfloat16)
    return jnp.concatenate([high, middle, low], axis=0)


def joined(stacked, count):
    return stacked[:count] + (stacked[count : 2 * count] + stacked[2 * count :])


def one_hot(cells, first):
    ids = lax.broadcasted_iota(jnp.int32, (WIDE, cells.shape[1]), 0) + first
    return jnp.where(ids == cells, 1.0, 0.0).astype(jnp.bfloat16)


def gather_kernel(cells_ref, field_ref, out_ref):
    count, width = field_ref.shape
    cells = cells_ref[...]

    def step(at, total):
        first = pl.multiple_of(at * WIDE, WIDE)
        stacked = split_rows(field_ref[:, pl.ds(first, WIDE)])
        return total + jnp.dot(stacked, one_hot(cells, first), preferred_element_type=jnp.float32)

    total = lax.fori_loop(
        0, width // WIDE, step, jnp.zeros((3 * count, cells.shape[1]), jnp.float32)
    )
    out_ref[...] = joined(total, count)


def scatter_kernel(cells_ref, flux_ref, out_ref):
    modes, width = out_ref.shape
    count = flux_ref.shape[0]
    cells = cells_ref[...]
    stacked = split_rows(flux_ref[...])

    @pl.loop(0, width // WIDE)
    def _(at):
        first = pl.multiple_of(at * WIDE, WIDE)
        spread = lax.dot_general(
            stacked,
            one_hot(cells, first),
            (((1,), (1,)), ((), ())),
            preferred_element_type=jnp.float32,
        )
        out_ref[:, pl.ds(first, WIDE)] = joined(spread, count)[:modes]


def group_of(modes):
    return 8 if modes % 8 == 0 else 4


def mix_kernel(modes, slots, random_terms, with_before, with_faces, previous, *refs):
    refs = list(refs)
    take = lambda count: [refs.pop(0) for _ in range(count)]
    partner_ref, weight_ref, coef_ref = take(3)
    parts = take(slots)
    before_ref = take(1)[0] if with_before else None
    face_coef_ref = take(1)[0] if with_faces else None
    face_parts = take(slots) if with_faces else []
    if previous:
        done = take(previous)
        uppers = take(previous)
        face_ref, alive_ref = take(2)
    out_ref, = take(1)
    if not previous:
        upper_ref, lower_ref = take(2)
    flux_ref = take(1)[0] if with_faces else None
    held, result, upper_own, lower_own = take(4)
    if with_faces:
        face_held, face_result = take(2)
    group = group_of(modes)

    for part_list, target, count in ((parts, held, ROWS), (face_parts, face_held if with_faces else None, 4)):
        for slot, part in enumerate(part_list):
            for first in range(0, modes, group):
                for row in range(count):
                    target[pl.ds((slot * modes + first) * ROWS + row, group, stride=ROWS), :] = part[
                        first : first + group, row * GZ : (row + 1) * GZ
                    ]

    row_ids = lax.broadcasted_iota(jnp.int32, (ROWS, GZ), 0)

    @pl.loop(0, modes // TOGETHER)
    def _(turn):
        sums = [[None] * 5 for _ in range(TOGETHER)]

        def add(at, which, value):
            old = sums[at][which]
            sums[at][which] = value if old is None else old + value

        for term in range(random_terms + 1):
            coefs = [coef_ref[which, term] for which in range(4)]
            face_coef = face_coef_ref[term] if with_faces else None
            for at in range(TOGETHER):
                mode = turn * TOGETHER + at
                if term == 0:
                    own = pl.multiple_of(mode * ROWS, ROWS)
                    mixed = held[pl.ds(own, ROWS), :]
                    if with_faces:
                        face_mixed = face_held[pl.ds(own, 4), :]
                else:
                    base = 2 * (term - 1)
                    one = pl.multiple_of(partner_ref[base, mode], ROWS)
                    two = pl.multiple_of(partner_ref[base + 1, mode], ROWS)
                    weight_one = weight_ref[base, mode]
                    weight_two = weight_ref[base + 1, mode]
                    mixed = weight_one * held[pl.ds(one, ROWS), :] + weight_two * held[pl.ds(two, ROWS), :]
                    if with_faces:
                        face_mixed = (
                            weight_one * face_held[pl.ds(one, 4), :]
                            + weight_two * face_held[pl.ds(two, 4), :]
                        )
                for which in range(4):
                    add(at, which, coefs[which] * mixed)
                if with_faces:
                    add(at, 4, face_coef * face_mixed)
        for at in range(TOGETHER):
            mode = turn * TOGETHER + at
            own = pl.multiple_of(mode * ROWS, ROWS)
            down, up, right, left, faces = sums[at]
            from_below = jnp.where(row_ids == ROWS - 1, 0.0, pltpu.roll(up, ROWS - 1, 0))
            from_above = jnp.where(row_ids == 0, 0.0, pltpu.roll(down, 1, 0))
            sideways = pltpu.roll(left, GZ - 1, 1) + pltpu.roll(right, 1, 1)
            result[pl.ds(own, ROWS), :] = (
                (down - from_below) + (up - from_above) + ((right + left) - sideways)
            )
            upper_own[pl.ds(mode, 1), :] = up[0:1]
            lower_own[pl.ds(mode, 1), :] = down[ROWS - 1 : ROWS]
            if with_faces:
                face_result[pl.ds(own, 4), :] = faces

    if with_faces:
        if flux_ref.shape[0] > modes:
            flux_ref[...] = jnp.zeros_like(flux_ref)
        for first in range(0, modes, group):
            for row in range(4):
                flux_ref[first : first + group, row * GZ : (row + 1) * GZ] = face_result[
                    pl.ds(first * ROWS + row, group, stride=ROWS), :
                ]
    offset = previous * CHUNK
    for first in range(0, modes, group):
        some = slice(first, first + group)
        for row in range(ROWS):
            value = result[pl.ds(first * ROWS + row, group, stride=ROWS), :]
            if row == 0 and with_before:
                value = value - before_ref[some, :]
            columns = slice(offset + row * GZ, offset + (row + 1) * GZ)
            if previous:
                value = (value + face_ref[some, columns]) * alive_ref[:, columns]
            out_ref[some, columns] = value
        if previous:
            for at in range(previous):
                for row in range(ROWS):
                    columns = slice(at * CHUNK + row * GZ, at * CHUNK + (row + 1) * GZ)
                    value = done[at][some, row * GZ : (row + 1) * GZ]
                    if row == ROWS - 1:
                        after = uppers[at + 1] if at + 1 < previous else upper_own
                        value = value - after[some, :]
                    out_ref[some, columns] = (value + face_ref[some, columns]) * alive_ref[:, columns]
    if not previous:
        upper_ref[...] = upper_own[...]
        lower_ref[...] = lower_own[...]


def spread_modes(value):
    count = lax.axis_size("mode")
    chips = count // 2
    sibling = [(source, source ^ 1) for source in range(count)]
    pieces = []
    for step in range(chips):
        if step == 0:
            direct = value
        else:
            direct = lax.ppermute(
                value,
                "mode",
                [((target + 2 * step) % count, target) for target in range(count)],
            )
        pieces.append(direct)
        pieces.append(lax.ppermute(direct, "mode", sibling))
    return pieces


def per_device(chaos_field, kl_field, partner, chaos_coef, cell_count, face_count, face_cells):
    modes, cells = chaos_field.shape
    rows_grid = cells // GZ
    chunks = cells // CHUNK
    random_terms = partner.shape[0]
    slots = lax.axis_size("mode")
    face_limit = face_cells.shape[2]
    faces = 4 * face_limit

    raw = [chaos_field[:, at * CHUNK : (at + 1) * CHUNK] for at in range(chunks)]
    gathered = [spread_modes(raw[0]), spread_modes(raw[1])]

    cells_flat = face_cells.reshape(1, faces)
    tall = modes + random_terms + 1
    padded = -(-tall // 16) * 16
    together = jnp.concatenate(
        [chaos_field, kl_field, jnp.zeros((padded - tall, cells), jnp.float32)], axis=0
    )
    own_values = pl.pallas_call(
        gather_kernel,
        out_shape=jax.ShapeDtypeStruct((padded, faces), jnp.float32),
        in_specs=[VMEM, VMEM],
        out_specs=VMEM,
        compiler_params=params(),
        cost_estimate=cost(4_000_000_000, 4 * padded * cells),
    )(cells_flat, together)
    outgoing = own_values[:tall]
    arrived = jnp.concatenate(
        [
            shifted(
                outgoing[:, (3 - slot) * face_limit : (4 - slot) * face_limit], "blk", -offset
            )
            for slot, offset in enumerate(SLOT_OFFSETS)
        ],
        axis=1,
    )
    face_alive = (
        (lax.iota(jnp.int32, face_limit)[None, :] < face_count[0][:, None])
        .astype(jnp.float32)
        .reshape(1, faces)
    )
    face_coef = 0.5 * (outgoing[modes:] + arrived[modes:]) * face_alive
    face_coef = face_coef.reshape(random_terms + 1, 4, face_limit)
    difference = outgoing[:modes] - arrived[:modes]

    alive_flag = (lax.iota(jnp.int32, cells) < cell_count[0]).astype(jnp.float32)
    alive = alive_flag.reshape(rows_grid, GZ)
    conduct = kl_field.reshape(random_terms + 1, rows_grid, GZ)
    down = 0.5 * (conduct[:, 1:] + conduct[:, :-1]) * (alive[1:] * alive[:-1])
    side = 0.5 * (conduct[:, :, 1:] + conduct[:, :, :-1]) * (alive[:, 1:] * alive[:, :-1])
    coefs = jnp.stack(
        [
            jnp.pad(down, ((0, 0), (0, 1), (0, 0))),
            jnp.pad(down, ((0, 0), (1, 0), (0, 0))),
            jnp.pad(side, ((0, 0), (0, 0), (0, 1))),
            jnp.pad(side, ((0, 0), (0, 0), (1, 0))),
        ]
    )

    me = lax.axis_index("mode")
    owner = partner // modes
    step = lax.rem(owner // 2 - me // 2 + slots // 2, slots // 2)
    slot = 2 * step + ((owner ^ me) & 1)
    places = ((slot * modes + lax.rem(partner, modes)) * ROWS).reshape(2 * random_terms, modes)
    weights = chaos_coef.reshape(2 * random_terms, modes)

    face_at = chunks - 2
    face_gathered = spread_modes(difference)
    padded_modes = -(-modes // 16) * 16
    results, uppers, before, face_add = [], [], None, None
    for at in range(chunks):
        last = at == chunks - 1
        with_faces = at == face_at
        if at >= 2:
            held_back, _ = lax.optimization_barrier((raw[at], gathered[at - 2][-2]))
            if last:
                held_back, _ = lax.optimization_barrier((held_back, difference))
            gathered.append(spread_modes(held_back))
        inputs = [places, weights, coefs[:, :, at * ROWS : (at + 1) * ROWS]] + gathered[at]
        in_specs = [SMEM, SMEM] + [VMEM] * (1 + slots)
        if at:
            inputs.append(before)
        if with_faces:
            inputs += [face_coef] + face_gathered
        if last:
            inputs += results + uppers + [face_add, alive_flag[None, :]]
        in_specs += [VMEM] * (len(inputs) - len(in_specs))
        edge = jax.ShapeDtypeStruct((modes, GZ), jnp.float32)
        if last:
            out_shape = [jax.ShapeDtypeStruct((modes, cells), jnp.float32)]
        else:
            out_shape = [jax.ShapeDtypeStruct((modes, CHUNK), jnp.float32), edge, edge]
        if with_faces:
            out_shape.append(jax.ShapeDtypeStruct((padded_modes, faces), jnp.float32))
        scratch = [
            pltpu.VMEM((slots * modes * ROWS, GZ), jnp.float32),
            pltpu.VMEM((modes * ROWS, GZ), jnp.float32),
            pltpu.VMEM((modes, GZ), jnp.float32),
            pltpu.VMEM((modes, GZ), jnp.float32),
        ]
        if with_faces:
            scratch += scratch[:2]
        outs = pl.pallas_call(
            functools.partial(
                mix_kernel, modes, slots, random_terms, at > 0, with_faces, at if last else 0
            ),
            out_shape=out_shape,
            in_specs=in_specs,
            out_specs=[VMEM] * len(out_shape),
            scratch_shapes=scratch,
            compiler_params=params(),
            cost_estimate=cost(5_000_000_000, 4 * slots * modes * CHUNK),
        )(*inputs)
        if last:
            return outs[0]
        results.append(outs[0])
        uppers.append(outs[1])
        before = outs[2]
        if with_faces:
            face_add = pl.pallas_call(
                scatter_kernel,
                out_shape=jax.ShapeDtypeStruct((modes, cells), jnp.float32),
                in_specs=[VMEM, VMEM],
                out_specs=VMEM,
                compiler_params=params(),
                cost_estimate=cost(4_000_000_000, 4 * modes * cells),
            )(cells_flat, outs[3])


def solution(mesh):
    in_specs = (
        P("mode", "blk"),
        P(None, "blk"),
        P(None, None, "mode"),
        P(None, None, "mode"),
        P("blk"),
        P("blk", None),
        P("blk", None, None),
    )
    return jax.shard_map(
        per_device, mesh=mesh, in_specs=in_specs, out_specs=P("mode", "blk"), check_vma=False
    )
```

```python
import functools

import jax
import jax.numpy as jnp
from jax import lax
from jax.experimental import pallas as pl
from jax.experimental.pallas import tpu as pltpu
from jax.sharding import PartitionSpec as P

GZ = 128
TILE = 8
WIDE = 256
TOGETHER = 4
SLOT_OFFSETS = (-2, -1, 1, 2)
VMEM = pl.BlockSpec(memory_space=pltpu.VMEM)
SMEM = pl.BlockSpec(memory_space=pltpu.SMEM)


def params():
    return pltpu.CompilerParams(vmem_limit_bytes=32 * 1024 * 1024)


def cost(flops, size):
    return pl.CostEstimate(flops=flops, bytes_accessed=size, transcendentals=0)


def split_rows(value):
    high = value.astype(jnp.bfloat16)
    low = (value - high.astype(jnp.float32)).astype(jnp.bfloat16)
    return jnp.concatenate([high, low], axis=0)


def joined(stacked, count):
    return stacked[:count] + stacked[count:]


def one_hot(cells, first):
    ids = lax.broadcasted_iota(jnp.int32, (WIDE, cells.shape[1]), 0) + first
    return jnp.where(ids == cells, 1.0, 0.0).astype(jnp.bfloat16)


def chunk_rows(rows_grid):
    half = rows_grid // 2 // TILE * TILE
    rest = rows_grid - half
    return [half] + [TILE] * (rest // TILE)


def relayout_kernel(sizes, field_ref, *out_refs):
    modes = field_ref.shape[0]
    group = group_of(modes)
    start = 0
    for size, out_ref in zip(sizes, out_refs):
        for first in range(0, modes, group):
            for row in range(size):
                columns = slice((start + row) * GZ, (start + row + 1) * GZ)
                out_ref[pl.ds(first * size + row, group, stride=size), :] = field_ref[
                    first : first + group, columns
                ]
        start += size


def face_kernel(
    count, lead, cells_ref, field_ref, kl_ref, out_ref, conduct_ref, both, own, arrived, send, recv
):
    modes, width = field_ref.shape
    padded = both.shape[0]
    limit = own.shape[2]
    me = lax.axis_index("blk")
    barrier = pltpu.get_barrier_semaphore()
    exists, copies = [], []
    for slot, offset in enumerate(SLOT_OFFSETS):
        there = (me + offset >= 0) & (me + offset < count)
        exists.append(there)
        copies.append(
            pltpu.make_async_remote_copy(
                src_ref=own.at[slot],
                dst_ref=arrived.at[3 - slot],
                send_sem=send.at[slot],
                recv_sem=recv.at[3 - slot],
                device_id={"blk": me + offset},
                device_id_type=pl.DeviceIdType.MESH,
            )
        )

        @pl.when(there)
        def _():
            pl.semaphore_signal(
                barrier,
                inc=1,
                device_id={"blk": me + offset},
                device_id_type=pl.DeviceIdType.MESH,
            )

    both[...] = jnp.zeros_like(both)
    both[: kl_ref.shape[0], :] = kl_ref[...]
    both[lead : lead + modes, :] = field_ref[...]
    cells = cells_ref[...]

    def step(at, total):
        first = pl.multiple_of(at * WIDE, WIDE)
        stacked = split_rows(both[:, pl.ds(first, WIDE)])
        return total + jnp.dot(stacked, one_hot(cells, first), preferred_element_type=jnp.float32)

    total = lax.fori_loop(
        0, width // WIDE, step, jnp.zeros((2 * padded, cells.shape[1]), jnp.float32)
    )
    values = joined(total, padded)
    for slot in range(4):
        own[slot] = values[:, slot * limit : (slot + 1) * limit]

    pl.semaphore_wait(barrier, sum(there.astype(jnp.int32) for there in exists))

    for slot in range(4):
        @pl.when(exists[slot])
        def _():
            copies[slot].start()

        @pl.when(jnp.logical_not(exists[slot]))
        def _():
            arrived[slot] = jnp.zeros_like(arrived[slot])

    for slot in range(4):
        @pl.when(exists[slot])
        def _():
            copies[slot].wait_send()
            pltpu.make_async_remote_copy(
                src_ref=own.at[slot],
                dst_ref=arrived.at[slot],
                send_sem=send.at[slot],
                recv_sem=recv.at[slot],
                device_id={"blk": me + SLOT_OFFSETS[slot]},
                device_id_type=pl.DeviceIdType.MESH,
            ).wait_recv()

    for slot in range(4):
        out_ref[:, slot * limit : (slot + 1) * limit] = (
            own[slot, lead : lead + modes, :] - arrived[slot, lead : lead + modes, :]
        )
        conduct_ref[slot] = own[slot, :lead, :] + arrived[slot, :lead, :]


def scatter_kernel(cells_ref, flux_ref, out_ref):
    modes, width = out_ref.shape
    count = flux_ref.shape[0]
    cells = cells_ref[...]
    stacked = split_rows(flux_ref[...])

    @pl.loop(0, width // WIDE)
    def _(at):
        first = pl.multiple_of(at * WIDE, WIDE)
        spread = lax.dot_general(
            stacked,
            one_hot(cells, first),
            (((1,), (1,)), ((), ())),
            preferred_element_type=jnp.float32,
        )
        out_ref[:, pl.ds(first, WIDE)] = joined(spread, count)[:modes]


def group_of(modes):
    return 8 if modes % 8 == 0 else 4


def mix_kernel(modes, slots, random_terms, rows, with_before, with_faces, earlier, *refs):
    previous = len(earlier)
    refs = list(refs)
    take = lambda count: [refs.pop(0) for _ in range(count)]
    partner_ref, weight_ref, coef_ref = take(3)
    parts = take(slots)
    before_ref = take(1)[0] if with_before else None
    face_coef_ref = take(1)[0] if with_faces else None
    face_parts = take(slots) if with_faces else []
    if previous:
        done = take(previous)
        uppers = take(previous)
        face_ref, alive_ref = take(2)
    out_ref, = take(1)
    if not previous:
        upper_ref, lower_ref = take(2)
    flux_ref = take(1)[0] if with_faces else None
    held, result, upper_own, lower_own = take(4)
    if with_faces:
        face_held, face_result = take(2)
    group = group_of(modes)

    size = modes * rows
    for slot, part in enumerate(parts):
        held[slot * size : (slot + 1) * size, :] = part[...]
    for slot, part in enumerate(face_parts):
        for first in range(0, modes, group):
            for row in range(4):
                face_held[pl.ds((slot * modes + first) * rows + row, group, stride=rows), :] = part[
                    first : first + group, row * GZ : (row + 1) * GZ
                ]

    row_ids = lax.broadcasted_iota(jnp.int32, (rows, GZ), 0)

    @pl.loop(0, modes // TOGETHER)
    def _(turn):
        sums = [[None] * 5 for _ in range(TOGETHER)]

        def add(at, which, value):
            old = sums[at][which]
            sums[at][which] = value if old is None else old + value

        for term in range(random_terms + 1):
            coefs = [coef_ref[which, term] for which in range(4)]
            face_coef = face_coef_ref[term] if with_faces else None
            for at in range(TOGETHER):
                mode = turn * TOGETHER + at
                if term == 0:
                    own = pl.multiple_of(mode * rows, rows)
                    mixed = held[pl.ds(own, rows), :]
                    if with_faces:
                        face_mixed = face_held[pl.ds(own, 4), :]
                else:
                    base = 2 * (term - 1)
                    one = pl.multiple_of(partner_ref[base, mode], rows)
                    two = pl.multiple_of(partner_ref[base + 1, mode], rows)
                    weight_one = weight_ref[base, mode]
                    weight_two = weight_ref[base + 1, mode]
                    mixed = weight_one * held[pl.ds(one, rows), :] + weight_two * held[pl.ds(two, rows), :]
                    if with_faces:
                        face_mixed = (
                            weight_one * face_held[pl.ds(one, 4), :]
                            + weight_two * face_held[pl.ds(two, 4), :]
                        )
                for which in range(4):
                    add(at, which, coefs[which] * mixed)
                if with_faces:
                    add(at, 4, face_coef * face_mixed)
        for at in range(TOGETHER):
            mode = turn * TOGETHER + at
            own = pl.multiple_of(mode * rows, rows)
            down, up, right, left, faces = sums[at]
            from_below = jnp.where(row_ids == rows - 1, 0.0, pltpu.roll(up, rows - 1, 0))
            from_above = jnp.where(row_ids == 0, 0.0, pltpu.roll(down, 1, 0))
            sideways = pltpu.roll(left, GZ - 1, 1) + pltpu.roll(right, 1, 1)
            result[pl.ds(own, rows), :] = (
                (down - from_below) + (up - from_above) + ((right + left) - sideways)
            )
            upper_own[pl.ds(mode, 1), :] = up[0:1]
            lower_own[pl.ds(mode, 1), :] = down[rows - 1 : rows]
            if with_faces:
                face_result[pl.ds(own, 4), :] = faces

    if with_faces:
        if flux_ref.shape[0] > modes:
            flux_ref[...] = jnp.zeros_like(flux_ref)
        for first in range(0, modes, group):
            for row in range(4):
                flux_ref[first : first + group, row * GZ : (row + 1) * GZ] = face_result[
                    pl.ds(first * rows + row, group, stride=rows), :
                ]
    offset = sum(earlier) * GZ
    for first in range(0, modes, group):
        some = slice(first, first + group)
        for row in range(rows):
            value = result[pl.ds(first * rows + row, group, stride=rows), :]
            if row == 0 and with_before:
                value = value - before_ref[some, :]
            columns = slice(offset + row * GZ, offset + (row + 1) * GZ)
            if previous:
                value = (value + face_ref[some, columns]) * alive_ref[:, columns]
            out_ref[some, columns] = value
        start = 0
        for at in range(previous):
            for row in range(earlier[at]):
                columns = slice((start + row) * GZ, (start + row + 1) * GZ)
                value = done[at][some, row * GZ : (row + 1) * GZ]
                if row == earlier[at] - 1:
                    after = uppers[at + 1] if at + 1 < previous else upper_own
                    value = value - after[some, :]
                out_ref[some, columns] = (value + face_ref[some, columns]) * alive_ref[:, columns]
            start += earlier[at]
    if not previous:
        upper_ref[...] = upper_own[...]
        lower_ref[...] = lower_own[...]


def others(count):
    return [(source, source ^ 1) for source in range(count)]


def far_modes(value):
    count = lax.axis_size("mode")
    return [
        lax.ppermute(
            value, "mode", [((target + 2 * step) % count, target) for target in range(count)]
        )
        for step in range(1, count // 2)
    ]


def with_sibling(direct):
    pieces = []
    for value in direct:
        pieces += [value, lax.ppermute(value, "mode", others(lax.axis_size("mode")))]
    return pieces


def after(values, first):
    return list(lax.optimization_barrier((values, first))[0])


def per_device(chaos_field, kl_field, partner, chaos_coef, cell_count, face_count, face_cells):
    modes, cells = chaos_field.shape
    rows_grid = cells // GZ
    sizes = chunk_rows(rows_grid)
    chunks = len(sizes)
    random_terms = partner.shape[0]
    slots = lax.axis_size("mode")
    face_limit = face_cells.shape[2]
    faces = 4 * face_limit

    raw = pl.pallas_call(
        functools.partial(relayout_kernel, sizes),
        out_shape=[jax.ShapeDtypeStruct((modes * size, GZ), jnp.float32) for size in sizes],
        in_specs=[VMEM],
        out_specs=[VMEM] * chunks,
        compiler_params=params(),
        cost_estimate=cost(1_000_000_000, 8 * modes * cells),
    )(chaos_field)
    far = [far_modes(raw[0])]
    far.append(far_modes(raw[1]))

    cells_flat = face_cells.reshape(1, faces)
    lead = -(-(random_terms + 1) // 16) * 16
    padded = -(-(lead + modes) // 16) * 16
    difference, conduct_sum = pl.pallas_call(
        functools.partial(face_kernel, lax.axis_size("blk"), lead),
        out_shape=[
            jax.ShapeDtypeStruct((modes, faces), jnp.float32),
            jax.ShapeDtypeStruct((4, lead, face_limit), jnp.float32),
        ],
        in_specs=[VMEM] * 3,
        out_specs=[VMEM] * 2,
        scratch_shapes=[
            pltpu.VMEM((padded, cells), jnp.float32),
            pltpu.VMEM((4, padded, face_limit), jnp.float32),
            pltpu.VMEM((4, padded, face_limit), jnp.float32),
            pltpu.SemaphoreType.DMA((4,)),
            pltpu.SemaphoreType.DMA((4,)),
        ],
        compiler_params=pltpu.CompilerParams(
            vmem_limit_bytes=32 * 1024 * 1024, collective_id=0, has_side_effects=True
        ),
        cost_estimate=cost(8_000_000_000, 4 * padded * cells),
    )(cells_flat, chaos_field, kl_field)
    face_alive = (
        lax.iota(jnp.int32, face_limit)[None, :] < face_count[0][:, None]
    ).astype(jnp.float32)
    face_coef = jnp.transpose(0.5 * conduct_sum * face_alive[:, None, :], (1, 0, 2))
    face_coef = face_coef[: random_terms + 1]
    far_difference = far_modes(difference)

    alive_flag = (lax.iota(jnp.int32, cells) < cell_count[0]).astype(jnp.float32)
    alive = alive_flag.reshape(rows_grid, GZ)
    conduct = kl_field.reshape(random_terms + 1, rows_grid, GZ)
    down = 0.5 * (conduct[:, 1:] + conduct[:, :-1]) * (alive[1:] * alive[:-1])
    side = 0.5 * (conduct[:, :, 1:] + conduct[:, :, :-1]) * (alive[:, 1:] * alive[:, :-1])
    coefs = jnp.stack(
        [
            jnp.pad(down, ((0, 0), (0, 1), (0, 0))),
            jnp.pad(down, ((0, 0), (1, 0), (0, 0))),
            jnp.pad(side, ((0, 0), (0, 0), (0, 1))),
            jnp.pad(side, ((0, 0), (0, 0), (1, 0))),
        ]
    )

    me = lax.axis_index("mode")
    owner = partner // modes
    step = lax.rem(owner // 2 - me // 2 + slots // 2, slots // 2)
    slot = 2 * step + ((owner ^ me) & 1)
    places = (slot * modes + lax.rem(partner, modes)).reshape(2 * random_terms, modes)
    weights = chaos_coef.reshape(2 * random_terms, modes)

    face_at = chunks - 2
    padded_modes = -(-modes // 16) * 16
    results, uppers, before, face_add = [], [], None, None
    start = 0
    for at in range(chunks):
        last = at == chunks - 1
        with_faces = at == face_at
        rows = sizes[at]
        if at + 2 < chunks:
            later = after([raw[at + 2]], [far[at], difference])[0]
            far.append(far_modes(later))
        direct = after(far[at], results[-1]) if at else far[at]
        inputs = [places * rows, weights, coefs[:, :, start : start + rows]]
        inputs += with_sibling([raw[at]] + direct)
        in_specs = [SMEM, SMEM] + [VMEM] * (1 + slots)
        if at:
            inputs.append(before)
        if with_faces:
            far_faces = after(far_difference, results[-1]) if at else far_difference
            inputs += [face_coef] + with_sibling([difference] + far_faces)
        if last:
            inputs += results + uppers + [face_add, alive_flag[None, :]]
        in_specs += [VMEM] * (len(inputs) - len(in_specs))
        edge = jax.ShapeDtypeStruct((modes, GZ), jnp.float32)
        if last:
            out_shape = [jax.ShapeDtypeStruct((modes, cells), jnp.float32)]
        else:
            out_shape = [jax.ShapeDtypeStruct((modes, rows * GZ), jnp.float32), edge, edge]
        if with_faces:
            out_shape.append(jax.ShapeDtypeStruct((padded_modes, faces), jnp.float32))
        scratch = [
            pltpu.VMEM((slots * modes * rows, GZ), jnp.float32),
            pltpu.VMEM((modes * rows, GZ), jnp.float32),
            pltpu.VMEM((modes, GZ), jnp.float32),
            pltpu.VMEM((modes, GZ), jnp.float32),
        ]
        if with_faces:
            scratch += scratch[:2]
        outs = pl.pallas_call(
            functools.partial(
                mix_kernel,
                modes,
                slots,
                random_terms,
                rows,
                at > 0,
                with_faces,
                sizes[:at] if last else [],
            ),
            out_shape=out_shape,
            in_specs=in_specs,
            out_specs=[VMEM] * len(out_shape),
            scratch_shapes=scratch,
            compiler_params=params(),
            cost_estimate=cost(6_000_000_000, 4 * slots * modes * rows * GZ),
        )(*inputs)
        if last:
            return outs[0]
        start += rows
        results.append(outs[0])
        uppers.append(outs[1])
        before = outs[2]
        if with_faces:
            face_add = pl.pallas_call(
                scatter_kernel,
                out_shape=jax.ShapeDtypeStruct((modes, cells), jnp.float32),
                in_specs=[VMEM, VMEM],
                out_specs=VMEM,
                compiler_params=params(),
                cost_estimate=cost(4_000_000_000, 4 * modes * cells),
            )(cells_flat, outs[3])


def solution(mesh):
    in_specs = (
        P("mode", "blk"),
        P(None, "blk"),
        P(None, None, "mode"),
        P(None, None, "mode"),
        P("blk"),
        P("blk", None),
        P("blk", None, None),
    )
    return jax.shard_map(
        per_device, mesh=mesh, in_specs=in_specs, out_specs=P("mode", "blk"), check_vma=False
    )
```

```python
import functools

import jax
import jax.numpy as jnp
from jax import lax
from jax.experimental import pallas as pl
from jax.experimental.pallas import tpu as pltpu
from jax.sharding import PartitionSpec as P

GZ = 128
TILE = 8
WIDE = 256
TOGETHER = 4
SLOT_OFFSETS = (-2, -1, 1, 2)
VMEM = pl.BlockSpec(memory_space=pltpu.VMEM)
SMEM = pl.BlockSpec(memory_space=pltpu.SMEM)


def params():
    return pltpu.CompilerParams(vmem_limit_bytes=32 * 1024 * 1024)


def cost(flops, size):
    return pl.CostEstimate(flops=flops, bytes_accessed=size, transcendentals=0)


def split_rows(value):
    high = value.astype(jnp.bfloat16)
    low = (value - high.astype(jnp.float32)).astype(jnp.bfloat16)
    return jnp.concatenate([high, low], axis=0)


def joined(stacked, count):
    return stacked[:count] + stacked[count:]


def one_hot(cells, first):
    ids = lax.broadcasted_iota(jnp.int32, (WIDE, cells.shape[1]), 0) + first
    return jnp.where(ids == cells, 1.0, 0.0).astype(jnp.bfloat16)


def chunk_rows(rows_grid):
    half = rows_grid // 2 // TILE * TILE
    return [half, rows_grid - half]


def relayout_kernel(sizes, field_ref, *out_refs):
    modes = field_ref.shape[0]
    group = group_of(modes)
    start = 0
    for size, out_ref in zip(sizes, out_refs):
        for first in range(0, modes, group):
            for row in range(size):
                columns = slice((start + row) * GZ, (start + row + 1) * GZ)
                out_ref[pl.ds(first * size + row, group, stride=size), :] = field_ref[
                    first : first + group, columns
                ]
        start += size


def face_kernel(
    count, lead, cells_ref, field_ref, kl_ref, out_ref, conduct_ref, both, own, arrived, send, recv
):
    modes, width = field_ref.shape
    padded = both.shape[0]
    limit = own.shape[2]
    me = lax.axis_index("blk")
    barrier = pltpu.get_barrier_semaphore()
    exists, copies = [], []
    for slot, offset in enumerate(SLOT_OFFSETS):
        there = (me + offset >= 0) & (me + offset < count)
        exists.append(there)
        copies.append(
            pltpu.make_async_remote_copy(
                src_ref=own.at[slot],
                dst_ref=arrived.at[3 - slot],
                send_sem=send.at[slot],
                recv_sem=recv.at[3 - slot],
                device_id={"blk": me + offset},
                device_id_type=pl.DeviceIdType.MESH,
            )
        )

        @pl.when(there)
        def _():
            pl.semaphore_signal(
                barrier,
                inc=1,
                device_id={"blk": me + offset},
                device_id_type=pl.DeviceIdType.MESH,
            )

    both[...] = jnp.zeros_like(both)
    both[: kl_ref.shape[0], :] = kl_ref[...]
    both[lead : lead + modes, :] = field_ref[...]
    cells = cells_ref[...]

    def step(at, total):
        first = pl.multiple_of(at * WIDE, WIDE)
        stacked = split_rows(both[:, pl.ds(first, WIDE)])
        return total + jnp.dot(stacked, one_hot(cells, first), preferred_element_type=jnp.float32)

    total = lax.fori_loop(
        0, width // WIDE, step, jnp.zeros((2 * padded, cells.shape[1]), jnp.float32)
    )
    values = joined(total, padded)
    for slot in range(4):
        own[slot] = values[:, slot * limit : (slot + 1) * limit]

    pl.semaphore_wait(barrier, sum(there.astype(jnp.int32) for there in exists))

    for slot in range(4):
        @pl.when(exists[slot])
        def _():
            copies[slot].start()

        @pl.when(jnp.logical_not(exists[slot]))
        def _():
            arrived[slot] = jnp.zeros_like(arrived[slot])

    for slot in range(4):
        @pl.when(exists[slot])
        def _():
            copies[slot].wait_send()
            pltpu.make_async_remote_copy(
                src_ref=own.at[slot],
                dst_ref=arrived.at[slot],
                send_sem=send.at[slot],
                recv_sem=recv.at[slot],
                device_id={"blk": me + SLOT_OFFSETS[slot]},
                device_id_type=pl.DeviceIdType.MESH,
            ).wait_recv()

    for slot in range(4):
        out_ref[:, slot * limit : (slot + 1) * limit] = (
            own[slot, lead : lead + modes, :] - arrived[slot, lead : lead + modes, :]
        )
        conduct_ref[slot] = own[slot, :lead, :] + arrived[slot, :lead, :]


def scatter_kernel(cells_ref, flux_ref, out_ref):
    modes, width = out_ref.shape
    count = flux_ref.shape[0]
    cells = cells_ref[...]
    stacked = split_rows(flux_ref[...])

    @pl.loop(0, width // WIDE)
    def _(at):
        first = pl.multiple_of(at * WIDE, WIDE)
        spread = lax.dot_general(
            stacked,
            one_hot(cells, first),
            (((1,), (1,)), ((), ())),
            preferred_element_type=jnp.float32,
        )
        out_ref[:, pl.ds(first, WIDE)] = joined(spread, count)[:modes]


def group_of(modes):
    return 8 if modes % 8 == 0 else 4


def mix_kernel(modes, slots, random_terms, rows, with_before, with_faces, earlier, *refs):
    previous = len(earlier)
    refs = list(refs)
    take = lambda count: [refs.pop(0) for _ in range(count)]
    partner_ref, weight_ref, coef_ref = take(3)
    parts = take(slots)
    before_ref = take(1)[0] if with_before else None
    face_coef_ref = take(1)[0] if with_faces else None
    face_parts = take(slots) if with_faces else []
    if previous:
        done = take(previous)
        uppers = take(previous)
        face_ref, alive_ref = take(2)
    out_ref, = take(1)
    if not previous:
        upper_ref, lower_ref = take(2)
    flux_ref = take(1)[0] if with_faces else None
    held, result, upper_own, lower_own = take(4)
    if with_faces:
        face_held, face_result = take(2)
    group = group_of(modes)

    size = modes * rows
    for slot, part in enumerate(parts):
        held[slot * size : (slot + 1) * size, :] = part[...]
    for slot, part in enumerate(face_parts):
        for first in range(0, modes, group):
            for row in range(4):
                face_held[pl.ds((slot * modes + first) * rows + row, group, stride=rows), :] = part[
                    first : first + group, row * GZ : (row + 1) * GZ
                ]

    row_ids = lax.broadcasted_iota(jnp.int32, (rows, GZ), 0)

    @pl.loop(0, modes // TOGETHER)
    def _(turn):
        sums = [[None] * 5 for _ in range(TOGETHER)]

        def add(at, which, value):
            old = sums[at][which]
            sums[at][which] = value if old is None else old + value

        for term in range(random_terms + 1):
            coefs = [coef_ref[which, term] for which in range(4)]
            face_coef = face_coef_ref[term] if with_faces else None
            for at in range(TOGETHER):
                mode = turn * TOGETHER + at
                if term == 0:
                    own = pl.multiple_of(mode * rows, rows)
                    mixed = held[pl.ds(own, rows), :]
                    if with_faces:
                        face_mixed = face_held[pl.ds(own, 4), :]
                else:
                    base = 2 * (term - 1)
                    one = pl.multiple_of(partner_ref[mode * (2 * random_terms) + base], rows)
                    two = pl.multiple_of(partner_ref[mode * (2 * random_terms) + base + 1], rows)
                    weight_one = weight_ref[mode, base : base + 1, :]
                    weight_two = weight_ref[mode, base + 1 : base + 2, :]
                    mixed = weight_one * held[pl.ds(one, rows), :] + weight_two * held[pl.ds(two, rows), :]
                    if with_faces:
                        face_mixed = (
                            weight_one * face_held[pl.ds(one, 4), :]
                            + weight_two * face_held[pl.ds(two, 4), :]
                        )
                for which in range(4):
                    add(at, which, coefs[which] * mixed)
                if with_faces:
                    add(at, 4, face_coef * face_mixed)
        for at in range(TOGETHER):
            mode = turn * TOGETHER + at
            own = pl.multiple_of(mode * rows, rows)
            down, up, right, left, faces = sums[at]
            from_below = jnp.where(row_ids == rows - 1, 0.0, pltpu.roll(up, rows - 1, 0))
            from_above = jnp.where(row_ids == 0, 0.0, pltpu.roll(down, 1, 0))
            sideways = pltpu.roll(left, GZ - 1, 1) + pltpu.roll(right, 1, 1)
            result[pl.ds(own, rows), :] = (
                (down - from_below) + (up - from_above) + ((right + left) - sideways)
            )
            upper_own[pl.ds(mode, 1), :] = up[0:1]
            lower_own[pl.ds(mode, 1), :] = down[rows - 1 : rows]
            if with_faces:
                face_result[pl.ds(own, 4), :] = faces

    if with_faces:
        if flux_ref.shape[0] > modes:
            flux_ref[...] = jnp.zeros_like(flux_ref)
        for first in range(0, modes, group):
            for row in range(4):
                flux_ref[first : first + group, row * GZ : (row + 1) * GZ] = face_result[
                    pl.ds(first * rows + row, group, stride=rows), :
                ]
    offset = sum(earlier) * GZ
    for first in range(0, modes, group):
        some = slice(first, first + group)
        for row in range(rows):
            value = result[pl.ds(first * rows + row, group, stride=rows), :]
            if row == 0 and with_before:
                value = value - before_ref[some, :]
            columns = slice(offset + row * GZ, offset + (row + 1) * GZ)
            if previous:
                value = (value + face_ref[some, columns]) * alive_ref[:, columns]
            out_ref[some, columns] = value
        start = 0
        for at in range(previous):
            for row in range(earlier[at]):
                columns = slice((start + row) * GZ, (start + row + 1) * GZ)
                value = done[at][some, row * GZ : (row + 1) * GZ]
                if row == earlier[at] - 1:
                    after = uppers[at + 1] if at + 1 < previous else upper_own
                    value = value - after[some, :]
                out_ref[some, columns] = (value + face_ref[some, columns]) * alive_ref[:, columns]
            start += earlier[at]
    if not previous:
        upper_ref[...] = upper_own[...]
        lower_ref[...] = lower_own[...]


def others(count):
    return [(source, source ^ 1) for source in range(count)]


def far_modes(value):
    count = lax.axis_size("mode")
    return [
        lax.ppermute(
            value, "mode", [((target + 2 * step) % count, target) for target in range(count)]
        )
        for step in range(1, count // 2)
    ]


def with_sibling(direct):
    pieces = []
    for value in direct:
        pieces += [value, lax.ppermute(value, "mode", others(lax.axis_size("mode")))]
    return pieces


def after(values, first):
    return list(lax.optimization_barrier((values, first))[0])


def per_device(chaos_field, kl_field, partner, chaos_coef, cell_count, face_count, face_cells):
    modes, cells = chaos_field.shape
    rows_grid = cells // GZ
    sizes = chunk_rows(rows_grid)
    chunks = len(sizes)
    random_terms = partner.shape[0]
    slots = lax.axis_size("mode")
    face_limit = face_cells.shape[2]
    faces = 4 * face_limit

    raw = pl.pallas_call(
        functools.partial(relayout_kernel, sizes),
        out_shape=[jax.ShapeDtypeStruct((modes * size, GZ), jnp.float32) for size in sizes],
        in_specs=[VMEM],
        out_specs=[VMEM] * chunks,
        compiler_params=params(),
        cost_estimate=cost(1_000_000_000, 8 * modes * cells),
    )(chaos_field)
    far = [far_modes(raw[0])]
    far.append(far_modes(after([raw[1]], far[0])[0]))

    cells_flat = after([face_cells.reshape(1, faces)], raw[0])[0]
    lead = -(-(random_terms + 1) // 16) * 16
    padded = -(-(lead + modes) // 16) * 16
    difference, conduct_sum = pl.pallas_call(
        functools.partial(face_kernel, lax.axis_size("blk"), lead),
        out_shape=[
            jax.ShapeDtypeStruct((modes, faces), jnp.float32),
            jax.ShapeDtypeStruct((4, lead, face_limit), jnp.float32),
        ],
        in_specs=[VMEM] * 3,
        out_specs=[VMEM] * 2,
        scratch_shapes=[
            pltpu.VMEM((padded, cells), jnp.float32),
            pltpu.VMEM((4, padded, face_limit), jnp.float32),
            pltpu.VMEM((4, padded, face_limit), jnp.float32),
            pltpu.SemaphoreType.DMA((4,)),
            pltpu.SemaphoreType.DMA((4,)),
        ],
        compiler_params=pltpu.CompilerParams(
            vmem_limit_bytes=32 * 1024 * 1024, collective_id=0, has_side_effects=True
        ),
        cost_estimate=cost(8_000_000_000, 4 * padded * cells),
    )(cells_flat, chaos_field, kl_field)
    face_alive = (
        lax.iota(jnp.int32, face_limit)[None, :] < face_count[0][:, None]
    ).astype(jnp.float32)
    face_coef = jnp.transpose(0.5 * conduct_sum * face_alive[:, None, :], (1, 0, 2))
    face_coef = face_coef[: random_terms + 1]
    far_difference = far_modes(difference)

    alive_flag = (lax.iota(jnp.int32, cells) < cell_count[0]).astype(jnp.float32)
    alive = alive_flag.reshape(rows_grid, GZ)
    conduct = kl_field.reshape(random_terms + 1, rows_grid, GZ)
    down = 0.5 * (conduct[:, 1:] + conduct[:, :-1]) * (alive[1:] * alive[:-1])
    side = 0.5 * (conduct[:, :, 1:] + conduct[:, :, :-1]) * (alive[:, 1:] * alive[:, :-1])
    coefs = jnp.stack(
        [
            jnp.pad(down, ((0, 0), (0, 1), (0, 0))),
            jnp.pad(down, ((0, 0), (1, 0), (0, 0))),
            jnp.pad(side, ((0, 0), (0, 0), (0, 1))),
            jnp.pad(side, ((0, 0), (0, 0), (1, 0))),
        ]
    )

    me = lax.axis_index("mode")
    owner = partner // modes
    step = lax.rem(owner // 2 - me // 2 + slots // 2, slots // 2)
    slot = 2 * step + ((owner ^ me) & 1)
    places = (slot * modes + lax.rem(partner, modes)).reshape(2 * random_terms, modes)
    places = places.T.reshape(-1)
    weights = chaos_coef.reshape(2 * random_terms, modes).T
    weights = jnp.broadcast_to(weights[:, :, None], weights.shape + (GZ,))

    face_at = chunks - 2
    padded_modes = -(-modes // 16) * 16
    results, uppers, before, face_add = [], [], None, None
    start = 0
    for at in range(chunks):
        last = at == chunks - 1
        with_faces = at == face_at
        rows = sizes[at]
        if at + 2 < chunks:
            later = after([raw[at + 2]], [far[at], difference])[0]
            far.append(far_modes(later))
        direct = after(far[at], face_add if last else results[-1]) if at else far[at]
        inputs = [places * rows, weights, coefs[:, :, start : start + rows]]
        inputs += with_sibling([raw[at]] + direct)
        in_specs = [SMEM] + [VMEM] * (2 + slots)
        if at:
            inputs.append(before)
        if with_faces:
            far_faces = after(far_difference, results[-1]) if at else far_difference
            inputs += [face_coef] + with_sibling([difference] + far_faces)
        if last:
            inputs += results + uppers + [face_add, alive_flag[None, :]]
        in_specs += [VMEM] * (len(inputs) - len(in_specs))
        edge = jax.ShapeDtypeStruct((modes, GZ), jnp.float32)
        if last:
            out_shape = [jax.ShapeDtypeStruct((modes, cells), jnp.float32)]
        else:
            out_shape = [jax.ShapeDtypeStruct((modes, rows * GZ), jnp.float32), edge, edge]
        if with_faces:
            out_shape.append(jax.ShapeDtypeStruct((padded_modes, faces), jnp.float32))
        scratch = [
            pltpu.VMEM((slots * modes * rows, GZ), jnp.float32),
            pltpu.VMEM((modes * rows, GZ), jnp.float32),
            pltpu.VMEM((modes, GZ), jnp.float32),
            pltpu.VMEM((modes, GZ), jnp.float32),
        ]
        if with_faces:
            scratch += scratch[:2]
        outs = pl.pallas_call(
            functools.partial(
                mix_kernel,
                modes,
                slots,
                random_terms,
                rows,
                at > 0,
                with_faces,
                sizes[:at] if last else [],
            ),
            out_shape=out_shape,
            in_specs=in_specs,
            out_specs=[VMEM] * len(out_shape),
            scratch_shapes=scratch,
            compiler_params=params(),
            cost_estimate=cost(6_000_000_000, 4 * slots * modes * rows * GZ),
        )(*inputs)
        if last:
            return outs[0]
        start += rows
        results.append(outs[0])
        uppers.append(outs[1])
        before = outs[2]
        if with_faces:
            face_add = pl.pallas_call(
                scatter_kernel,
                out_shape=jax.ShapeDtypeStruct((modes, cells), jnp.float32),
                in_specs=[VMEM, VMEM],
                out_specs=VMEM,
                compiler_params=params(),
                cost_estimate=cost(4_000_000_000, 4 * modes * cells),
            )(cells_flat, outs[3])


def solution(mesh):
    in_specs = (
        P("mode", "blk"),
        P(None, "blk"),
        P(None, None, "mode"),
        P(None, None, "mode"),
        P("blk"),
        P("blk", None),
        P("blk", None, None),
    )
    return jax.shard_map(
        per_device, mesh=mesh, in_specs=in_specs, out_specs=P("mode", "blk"), check_vma=False
    )
```

```python
import functools

import jax
import jax.numpy as jnp
from jax import lax
from jax.experimental import pallas as pl
from jax.experimental.pallas import tpu as pltpu
from jax.sharding import PartitionSpec as P

GZ = 128
TILE = 8
WIDE = 256
TOGETHER = 4
SLOT_OFFSETS = (-2, -1, 1, 2)
VMEM = pl.BlockSpec(memory_space=pltpu.VMEM)
SMEM = pl.BlockSpec(memory_space=pltpu.SMEM)


def params():
    return pltpu.CompilerParams(vmem_limit_bytes=32 * 1024 * 1024)


def cost(flops, size):
    return pl.CostEstimate(flops=flops, bytes_accessed=size, transcendentals=0)


def split_rows(value):
    high = value.astype(jnp.bfloat16)
    low = (value - high.astype(jnp.float32)).astype(jnp.bfloat16)
    return jnp.concatenate([high, low], axis=0)


def joined(stacked, count):
    return stacked[:count] + stacked[count:]


def one_hot(cells, first):
    ids = lax.broadcasted_iota(jnp.int32, (WIDE, cells.shape[1]), 0) + first
    return jnp.where(ids == cells, 1.0, 0.0).astype(jnp.bfloat16)


def chunk_rows(rows_grid):
    half = rows_grid // 2 // TILE * TILE
    return [half, rows_grid - half]


def relayout_kernel(sizes, field_ref, *out_refs):
    modes = field_ref.shape[0]
    group = group_of(modes)
    start = 0
    for size, out_ref in zip(sizes, out_refs):
        for first in range(0, modes, group):
            for row in range(size):
                columns = slice((start + row) * GZ, (start + row + 1) * GZ)
                out_ref[pl.ds(first * size + row, group, stride=size), :] = field_ref[
                    first : first + group, columns
                ]
        start += size


def face_kernel(
    count, lead, cells_ref, field_ref, kl_ref, out_ref, conduct_ref, both, own, arrived, send, recv
):
    modes, width = field_ref.shape
    padded = both.shape[0]
    limit = own.shape[2]
    me = lax.axis_index("blk")
    barrier = pltpu.get_barrier_semaphore()
    exists, copies = [], []
    for slot, offset in enumerate(SLOT_OFFSETS):
        there = (me + offset >= 0) & (me + offset < count)
        exists.append(there)
        copies.append(
            pltpu.make_async_remote_copy(
                src_ref=own.at[slot],
                dst_ref=arrived.at[3 - slot],
                send_sem=send.at[slot],
                recv_sem=recv.at[3 - slot],
                device_id={"blk": me + offset},
                device_id_type=pl.DeviceIdType.MESH,
            )
        )

        @pl.when(there)
        def _():
            pl.semaphore_signal(
                barrier,
                inc=1,
                device_id={"blk": me + offset},
                device_id_type=pl.DeviceIdType.MESH,
            )

    both[...] = jnp.zeros_like(both)
    both[: kl_ref.shape[0], :] = kl_ref[...]
    both[lead : lead + modes, :] = field_ref[...]
    cells = cells_ref[...]

    def step(at, total):
        first = pl.multiple_of(at * WIDE, WIDE)
        stacked = split_rows(both[:, pl.ds(first, WIDE)])
        return total + jnp.dot(stacked, one_hot(cells, first), preferred_element_type=jnp.float32)

    total = lax.fori_loop(
        0, width // WIDE, step, jnp.zeros((2 * padded, cells.shape[1]), jnp.float32)
    )
    values = joined(total, padded)
    for slot in range(4):
        own[slot] = values[:, slot * limit : (slot + 1) * limit]

    pl.semaphore_wait(barrier, sum(there.astype(jnp.int32) for there in exists))

    for slot in range(4):
        @pl.when(exists[slot])
        def _():
            copies[slot].start()

        @pl.when(jnp.logical_not(exists[slot]))
        def _():
            arrived[slot] = jnp.zeros_like(arrived[slot])

    for slot in range(4):
        @pl.when(exists[slot])
        def _():
            copies[slot].wait_send()
            pltpu.make_async_remote_copy(
                src_ref=own.at[slot],
                dst_ref=arrived.at[slot],
                send_sem=send.at[slot],
                recv_sem=recv.at[slot],
                device_id={"blk": me + SLOT_OFFSETS[slot]},
                device_id_type=pl.DeviceIdType.MESH,
            ).wait_recv()

    for slot in range(4):
        out_ref[:, slot * limit : (slot + 1) * limit] = (
            own[slot, lead : lead + modes, :] - arrived[slot, lead : lead + modes, :]
        )
        conduct_ref[slot] = own[slot, :lead, :] + arrived[slot, :lead, :]


def scatter_kernel(cells_ref, flux_ref, out_ref):
    modes, width = out_ref.shape
    count = flux_ref.shape[0]
    cells = cells_ref[...]
    stacked = split_rows(flux_ref[...])

    @pl.loop(0, width // WIDE)
    def _(at):
        first = pl.multiple_of(at * WIDE, WIDE)
        spread = lax.dot_general(
            stacked,
            one_hot(cells, first),
            (((1,), (1,)), ((), ())),
            preferred_element_type=jnp.float32,
        )
        out_ref[:, pl.ds(first, WIDE)] = joined(spread, count)[:modes]


def group_of(modes):
    return 8 if modes % 8 == 0 else 4


def mix_kernel(modes, slots, random_terms, rows, with_before, with_faces, earlier, *refs):
    previous = len(earlier)
    refs = list(refs)
    take = lambda count: [refs.pop(0) for _ in range(count)]
    partner_ref, weight_ref, coef_ref = take(3)
    parts = take(slots)
    before_ref = take(1)[0] if with_before else None
    face_coef_ref = take(1)[0] if with_faces else None
    face_parts = take(slots) if with_faces else []
    if previous:
        done = take(previous)
        uppers = take(previous)
        face_ref, alive_ref = take(2)
    out_ref, = take(1)
    if not previous:
        upper_ref, lower_ref = take(2)
    flux_ref = take(1)[0] if with_faces else None
    held, result, upper_own, lower_own = take(4)
    if with_faces:
        face_held, face_result = take(2)
    group = group_of(modes)

    size = modes * rows
    for slot, part in enumerate(parts):
        held[slot * size : (slot + 1) * size, :] = part[...]
    for slot, part in enumerate(face_parts):
        for first in range(0, modes, group):
            for row in range(4):
                face_held[pl.ds((slot * modes + first) * rows + row, group, stride=rows), :] = part[
                    first : first + group, row * GZ : (row + 1) * GZ
                ]

    row_ids = lax.broadcasted_iota(jnp.int32, (rows, GZ), 0)

    @pl.loop(0, modes // TOGETHER)
    def _(turn):
        sums = [[None] * 5 for _ in range(TOGETHER)]

        def add(at, which, value):
            old = sums[at][which]
            sums[at][which] = value if old is None else old + value

        for term in range(random_terms + 1):
            coefs = [coef_ref[which, term] for which in range(4)]
            face_coef = face_coef_ref[term] if with_faces else None
            for at in range(TOGETHER):
                mode = turn * TOGETHER + at
                if term == 0:
                    own = pl.multiple_of(mode * rows, rows)
                    mixed = held[pl.ds(own, rows), :]
                    if with_faces:
                        face_mixed = face_held[pl.ds(own, 4), :]
                else:
                    base = 2 * (term - 1)
                    one = pl.multiple_of(partner_ref[mode * (2 * random_terms) + base], rows)
                    two = pl.multiple_of(partner_ref[mode * (2 * random_terms) + base + 1], rows)
                    weight_one = weight_ref[mode * (2 * random_terms) + base]
                    weight_two = weight_ref[mode * (2 * random_terms) + base + 1]
                    mixed = weight_one * held[pl.ds(one, rows), :] + weight_two * held[pl.ds(two, rows), :]
                    if with_faces:
                        face_mixed = (
                            weight_one * face_held[pl.ds(one, 4), :]
                            + weight_two * face_held[pl.ds(two, 4), :]
                        )
                for which in range(4):
                    add(at, which, coefs[which] * mixed)
                if with_faces:
                    add(at, 4, face_coef * face_mixed)
        for at in range(TOGETHER):
            mode = turn * TOGETHER + at
            own = pl.multiple_of(mode * rows, rows)
            down, up, right, left, faces = sums[at]
            from_below = jnp.where(row_ids == rows - 1, 0.0, pltpu.roll(up, rows - 1, 0))
            from_above = jnp.where(row_ids == 0, 0.0, pltpu.roll(down, 1, 0))
            sideways = pltpu.roll(left, GZ - 1, 1) + pltpu.roll(right, 1, 1)
            result[pl.ds(own, rows), :] = (
                (down - from_below) + (up - from_above) + ((right + left) - sideways)
            )
            upper_own[pl.ds(mode, 1), :] = up[0:1]
            lower_own[pl.ds(mode, 1), :] = down[rows - 1 : rows]
            if with_faces:
                face_result[pl.ds(own, 4), :] = faces

    if with_faces:
        if flux_ref.shape[0] > modes:
            flux_ref[...] = jnp.zeros_like(flux_ref)
        for first in range(0, modes, group):
            for row in range(4):
                flux_ref[first : first + group, row * GZ : (row + 1) * GZ] = face_result[
                    pl.ds(first * rows + row, group, stride=rows), :
                ]
    offset = sum(earlier) * GZ
    for first in range(0, modes, group):
        some = slice(first, first + group)
        for row in range(rows):
            value = result[pl.ds(first * rows + row, group, stride=rows), :]
            if row == 0 and with_before:
                value = value - before_ref[some, :]
            columns = slice(offset + row * GZ, offset + (row + 1) * GZ)
            if previous:
                value = (value + face_ref[some, columns]) * alive_ref[:, columns]
            out_ref[some, columns] = value
        start = 0
        for at in range(previous):
            for row in range(earlier[at]):
                columns = slice((start + row) * GZ, (start + row + 1) * GZ)
                value = done[at][some, row * GZ : (row + 1) * GZ]
                if row == earlier[at] - 1:
                    after = uppers[at + 1] if at + 1 < previous else upper_own
                    value = value - after[some, :]
                out_ref[some, columns] = (value + face_ref[some, columns]) * alive_ref[:, columns]
            start += earlier[at]
    if not previous:
        upper_ref[...] = upper_own[...]
        lower_ref[...] = lower_own[...]


def others(count):
    return [(source, source ^ 1) for source in range(count)]


def far_modes(value):
    count = lax.axis_size("mode")
    return [
        lax.ppermute(
            value, "mode", [((target + 2 * step) % count, target) for target in range(count)]
        )
        for step in range(1, count // 2)
    ]


def with_sibling(direct):
    pieces = []
    for value in direct:
        pieces += [value, lax.ppermute(value, "mode", others(lax.axis_size("mode")))]
    return pieces


def after(values, first):
    return list(lax.optimization_barrier((values, first))[0])


def per_device(chaos_field, kl_field, partner, chaos_coef, cell_count, face_count, face_cells):
    modes, cells = chaos_field.shape
    rows_grid = cells // GZ
    sizes = chunk_rows(rows_grid)
    chunks = len(sizes)
    random_terms = partner.shape[0]
    slots = lax.axis_size("mode")
    face_limit = face_cells.shape[2]
    faces = 4 * face_limit

    raw = pl.pallas_call(
        functools.partial(relayout_kernel, sizes),
        out_shape=[jax.ShapeDtypeStruct((modes * size, GZ), jnp.float32) for size in sizes],
        in_specs=[VMEM],
        out_specs=[VMEM] * chunks,
        compiler_params=params(),
        cost_estimate=cost(1_000_000_000, 8 * modes * cells),
    )(chaos_field)
    far = [far_modes(raw[0])]

    cells_flat = after([face_cells.reshape(1, faces)], raw[0])[0]
    lead = -(-(random_terms + 1) // 16) * 16
    padded = -(-(lead + modes) // 16) * 16
    difference, conduct_sum = pl.pallas_call(
        functools.partial(face_kernel, lax.axis_size("blk"), lead),
        out_shape=[
            jax.ShapeDtypeStruct((modes, faces), jnp.float32),
            jax.ShapeDtypeStruct((4, lead, face_limit), jnp.float32),
        ],
        in_specs=[VMEM] * 3,
        out_specs=[VMEM] * 2,
        scratch_shapes=[
            pltpu.VMEM((padded, cells), jnp.float32),
            pltpu.VMEM((4, padded, face_limit), jnp.float32),
            pltpu.VMEM((4, padded, face_limit), jnp.float32),
            pltpu.SemaphoreType.DMA((4,)),
            pltpu.SemaphoreType.DMA((4,)),
        ],
        compiler_params=pltpu.CompilerParams(
            vmem_limit_bytes=32 * 1024 * 1024, collective_id=0, has_side_effects=True
        ),
        cost_estimate=cost(8_000_000_000, 4 * padded * cells),
    )(cells_flat, chaos_field, kl_field)
    face_alive = (
        lax.iota(jnp.int32, face_limit)[None, :] < face_count[0][:, None]
    ).astype(jnp.float32)
    face_coef = jnp.transpose(0.5 * conduct_sum * face_alive[:, None, :], (1, 0, 2))
    face_coef = face_coef[: random_terms + 1]
    held_difference, held_next = after([difference, raw[1]], far[0])
    far_difference = far_modes(held_difference)
    far.append(far_modes(held_next))

    alive_flag = (lax.iota(jnp.int32, cells) < cell_count[0]).astype(jnp.float32)
    alive = alive_flag.reshape(rows_grid, GZ)
    conduct = kl_field.reshape(random_terms + 1, rows_grid, GZ)
    down = 0.5 * (conduct[:, 1:] + conduct[:, :-1]) * (alive[1:] * alive[:-1])
    side = 0.5 * (conduct[:, :, 1:] + conduct[:, :, :-1]) * (alive[:, 1:] * alive[:, :-1])
    coefs = jnp.stack(
        [
            jnp.pad(down, ((0, 0), (0, 1), (0, 0))),
            jnp.pad(down, ((0, 0), (1, 0), (0, 0))),
            jnp.pad(side, ((0, 0), (0, 0), (0, 1))),
            jnp.pad(side, ((0, 0), (0, 0), (1, 0))),
        ]
    )

    me = lax.axis_index("mode")
    owner = partner // modes
    step = lax.rem(owner // 2 - me // 2 + slots // 2, slots // 2)
    slot = 2 * step + ((owner ^ me) & 1)
    places = (slot * modes + lax.rem(partner, modes)).reshape(2 * random_terms, modes)
    places = places.T.reshape(-1)
    weights = chaos_coef.reshape(2 * random_terms, modes).T.reshape(-1)

    face_at = chunks - 2
    padded_modes = -(-modes // 16) * 16
    results, uppers, before, face_add = [], [], None, None
    start = 0
    for at in range(chunks):
        last = at == chunks - 1
        with_faces = at == face_at
        rows = sizes[at]
        if at + 2 < chunks:
            later = after([raw[at + 2]], [far[at], difference])[0]
            far.append(far_modes(later))
        direct = after(far[at], face_add if last else results[-1]) if at else far[at]
        inputs = [places * rows, weights, coefs[:, :, start : start + rows]]
        inputs += with_sibling([raw[at]] + direct)
        in_specs = [SMEM, SMEM] + [VMEM] * (1 + slots)
        if at:
            inputs.append(before)
        if with_faces:
            far_faces = after(far_difference, results[-1]) if at else far_difference
            inputs += [face_coef] + with_sibling([difference] + far_faces)
        if last:
            inputs += results + uppers + [face_add, alive_flag[None, :]]
        in_specs += [VMEM] * (len(inputs) - len(in_specs))
        edge = jax.ShapeDtypeStruct((modes, GZ), jnp.float32)
        if last:
            out_shape = [jax.ShapeDtypeStruct((modes, cells), jnp.float32)]
        else:
            out_shape = [jax.ShapeDtypeStruct((modes, rows * GZ), jnp.float32), edge, edge]
        if with_faces:
            out_shape.append(jax.ShapeDtypeStruct((padded_modes, faces), jnp.float32))
        scratch = [
            pltpu.VMEM((slots * modes * rows, GZ), jnp.float32),
            pltpu.VMEM((modes * rows, GZ), jnp.float32),
            pltpu.VMEM((modes, GZ), jnp.float32),
            pltpu.VMEM((modes, GZ), jnp.float32),
        ]
        if with_faces:
            scratch += scratch[:2]
        outs = pl.pallas_call(
            functools.partial(
                mix_kernel,
                modes,
                slots,
                random_terms,
                rows,
                at > 0,
                with_faces,
                sizes[:at] if last else [],
            ),
            out_shape=out_shape,
            in_specs=in_specs,
            out_specs=[VMEM] * len(out_shape),
            scratch_shapes=scratch,
            compiler_params=params(),
            cost_estimate=cost(6_000_000_000, 4 * slots * modes * rows * GZ),
        )(*inputs)
        if last:
            return outs[0]
        start += rows
        results.append(outs[0])
        uppers.append(outs[1])
        before = outs[2]
        if with_faces:
            face_add = pl.pallas_call(
                scatter_kernel,
                out_shape=jax.ShapeDtypeStruct((modes, cells), jnp.float32),
                in_specs=[VMEM, VMEM],
                out_specs=VMEM,
                compiler_params=params(),
                cost_estimate=cost(4_000_000_000, 4 * modes * cells),
            )(cells_flat, outs[3])


def solution(mesh):
    in_specs = (
        P("mode", "blk"),
        P(None, "blk"),
        P(None, None, "mode"),
        P(None, None, "mode"),
        P("blk"),
        P("blk", None),
        P("blk", None, None),
    )
    return jax.shard_map(
        per_device, mesh=mesh, in_specs=in_specs, out_specs=P("mode", "blk"), check_vma=False
    )
```
